32 devices in a mesh: elem: 8 (over z, x), lev: 4 (over y, core).
Axes of the slice: x: 2, y: 2, z: 4, core: 2. Of those that a mesh axis runs over, the one named last changes fastest.
Arguments:
- cloud_state: float32 [1024, 8, 4096], P(('elem', 'lev')), may hold values from -6 to 6
- substeps: int32 [1024], P('elem'), may hold values from 4 to 16
- element_links: int32 [256, 4], P('elem'), may hold values from 0 to 255, as said below
- host_state: float32 [4, 64, 4096], P(None, 'lev', 'elem'), may hold values from -6 to 6
- wind_field: float32 [2, 64, 4096], P(None, 'lev', 'elem'), may hold values from -3 to 3
- node_mass: float32 [4096], P('elem'), may hold values from 0.25 to 4
- field_coupling: float32 [8, 8], replicated, may hold values from -2 to 2
- force_map: float32 [8, 4], replicated, may hold values from -3 to 3
- feedback_map: float32 [4, 8], replicated, may hold values from -5 to 5
Outputs:
- cloud_new: float32 [1024, 8, 4096], P(('elem', 'lev'))
- host_new: float32 [4, 64, 4096], P(None, 'lev', 'elem')
The draws below stay inside these ranges and needn't reach their ends.
Inputs may be any that keep to these rules, and one draw needn't show every extreme that they name: `element_links`: the 256 elements form a doubly periodic grid of 16 rows in which each index of elem holds two neighbouring grid columns, all rows, in some order; element e lies on index e // 32 of elem. Entries 0 to 3 of row e give the global index of the element to the left, right, below and above element e. An element's right edge meets its right neighbour's left edge node for node (same j), its upper edge its upper neighbour's lower edge (same i). The left neighbour lies on the same index of elem or the one before it (cyclically), the right one on the same or the one after it, the lower and upper ones on the same index.
All inputs are finite; a program needn't handle non-finite values.
Results may differ from the reference program's by a relative error of at most 0.0003.
Values sent between devices are 32-bit elements; how exact they have to be, the bound alone decides.
A program may use at most 128 MiB of HBM per device.

```python
import math
import jax
import jax.numpy as jnp
import numpy as np
from jax import lax

FIELDS = 8
CRM_X = 64
LEVELS = 64
HVARS = 4
SUB_MIN = 4
SUB_MAX = 16
COL_DEV = 128
COLS = 1024
ELEM_DEV = 32
ELEMS = 256
ELEM_ROWS = 16
NODES = 4096
CELLS = 4096
N_ELEM = 8


def draw_substeps(key, part):
    heavy_rank = jax.random.permutation(jax.random.fold_in(key, 21), N_ELEM)
    heavy_rows = heavy_rank < max(1, N_ELEM // 8)
    strong_counts = jax.random.randint(jax.random.fold_in(key, 22), (N_ELEM, COL_DEV), SUB_MAX - 3, SUB_MAX + 1)
    weak_counts = jax.random.randint(jax.random.fold_in(key, 23), (N_ELEM, COL_DEV), SUB_MIN, SUB_MIN + 3)
    counts = jnp.where(heavy_rows[:, None], strong_counts, weak_counts)
    counts = counts.at[:, 0].set(jnp.where(heavy_rows, SUB_MAX, SUB_MIN))
    return counts.reshape(COLS).astype(jnp.int32)


def draw_element_links(key, part):
    device_keys = jax.random.split(jax.random.fold_in(key, 31), N_ELEM)
    placed = jax.vmap(lambda single: jax.random.permutation(single, ELEM_DEV))(device_keys)
    stored = jnp.argsort(placed, axis=1)
    device = jnp.arange(N_ELEM)[:, None]
    row_of = placed // 2
    side_of = placed % 2

    def global_id(dev_index, row_index, side_index):
        dev_index = (dev_index + jnp.zeros_like(row_index)) % N_ELEM
        return dev_index * ELEM_DEV + stored[dev_index, row_index % ELEM_ROWS * 2 + side_index]
    left_ids = jnp.where(side_of == 1, global_id(device, row_of, 0), global_id(device - 1, row_of, 1))
    right_ids = jnp.where(side_of == 0, global_id(device, row_of, 1), global_id(device + 1, row_of, 0))
    lower_ids = global_id(device, row_of - 1, side_of)
    upper_ids = global_id(device, row_of + 1, side_of)
    return jnp.stack([left_ids, right_ids, lower_ids, upper_ids], axis=-1).reshape(ELEMS, 4).astype(jnp.int32)


def level_of(stream_key, extent, pieces, smallest, high):
    factor_of = 1.0
    for dim, parts in pieces:
        heights = jax.random.uniform(jax.random.fold_in(jax.random.fold_in(stream_key, 6), dim), (parts,), jnp.float32, smallest / len(pieces), high / len(pieces))
        factor_of = factor_of * jnp.repeat(jnp.exp(heights), extent[dim] // parts).reshape((-1,) + (1,) * (len(extent) - 1 - dim))
    return factor_of


def normal_values(own_key, extent, width, bound, pieces=(), kind=jnp.bfloat16):
    result = width * jax.random.normal(own_key, extent, jnp.float32)
    if pieces:
        result = result * level_of(own_key, extent, pieces, -0.22, 0.18)
    return jnp.clip(result, -bound, bound).astype(kind)


def setup_inputs(seed: int = 0) -> dict:
    splits = jax.random.split(jax.random.key(seed), 10)
    return {
        "cloud_state": normal_values(splits[0], (COLS, FIELDS, CELLS), 1.0, 6.0, ((0, 32),), jnp.float32),
        "substeps": draw_substeps(jax.random.fold_in(splits[9], 71), 0),
        "element_links": draw_element_links(jax.random.fold_in(splits[9], 71), 0),
        "host_state": normal_values(splits[3], (HVARS, LEVELS, NODES), 1.0, 6.0, ((1, 4), (2, 8)), jnp.float32),
        "wind_field": normal_values(splits[4], (2, LEVELS, NODES), 0.5, 3.0, ((1, 4), (2, 8)), jnp.float32),
        "node_mass": jnp.clip(jnp.exp(math.log(4.0) - 2.7725887 * jax.random.uniform(splits[5], (NODES,), jnp.float32) ** level_of(splits[5], (NODES,), ((0, 8),), -0.2, 0.2)), 0.25, 4.0),
        "field_coupling": normal_values(splits[6], (FIELDS, FIELDS), FIELDS ** -0.5, 2.0, (), jnp.float32),
        "force_map": normal_values(splits[7], (FIELDS, HVARS), HVARS ** -0.5, 3.0, (), jnp.float32),
        "feedback_map": normal_values(splits[8], (HVARS, FIELDS), 1.0, 5.0, (), jnp.float32),
    }


lateral_mix = 0.2
vertical_mix = 0.2
cloud_step = 0.1
host_step = 0.1
host_mix = 0.2
highest = lax.Precision.HIGHEST

def gll_derivative():
    points = np.array([-1.0, -1.0 / np.sqrt(5.0), 1.0 / np.sqrt(5.0), 1.0])
    weights = np.array([1.0 / np.prod([points[index] - points[other] for other in range(4) if other != index]) for index in range(4)])
    matrix = np.zeros((4, 4))
    for target in range(4):
        for source in range(4):
            if target != source:
                matrix[target, source] = weights[source] / weights[target] / (points[target] - points[source])
        matrix[target, target] = -np.sum(matrix[target])
    return matrix

def run_clouds(cloud_state, driving, substeps, field_coupling):

    def advance(packed):
        column, forcing, count = packed
        spread = jnp.repeat(forcing, CRM_X, axis=1)
        for stepno in range(SUB_MAX):
            padded = jnp.pad(column, ((0, 0), (CRM_X, CRM_X)))
            upper_cells = padded[:, 2 * CRM_X:]
            lower_cells = padded[:, :-2 * CRM_X]
            shaped = column.reshape(FIELDS, LEVELS, CRM_X)
            eastward = jnp.roll(shaped, -1, axis=2).reshape(column.shape)
            westward = jnp.roll(shaped, 1, axis=2).reshape(column.shape)
            reaction = jnp.tanh(jnp.dot(field_coupling, column, precision=highest))
            update = column + (lateral_mix * (eastward + westward - 2.0 * column) + vertical_mix * (upper_cells + lower_cells - 2.0 * column)) + cloud_step * (reaction + spread)
            column = jnp.where(stepno < count, update, column)
        return column
    return lax.map(advance, (cloud_state, driving, substeps))

def edge_sum(quantity, element_links):
    lead, levels, count = quantity.shape
    nodes_grid = quantity.reshape(lead, levels, count // 16, 4, 4)
    from_left = jnp.take(nodes_grid[..., 3], element_links[:, 0], axis=2)
    from_right = jnp.take(nodes_grid[..., 0], element_links[:, 1], axis=2)
    nodes_grid = nodes_grid.at[..., 0].add(from_left).at[..., 3].add(from_right)
    tops = nodes_grid[..., 3, :]
    bottoms = nodes_grid[..., 0, :]
    nodes_grid = nodes_grid.at[..., 0, :].add(jnp.take(tops, element_links[:, 2], axis=2)).at[..., 3, :].add(jnp.take(bottoms, element_links[:, 3], axis=2))
    return nodes_grid.reshape(lead, levels, count)

def reference(cloud_state, substeps, element_links, host_state, wind_field, node_mass, field_coupling, force_map, feedback_map):
    pooled = host_state.reshape(HVARS, LEVELS, ELEMS, 2, 2, 2, 2).mean(axis=(4, 6))
    host_columns = pooled.reshape(HVARS, LEVELS, COLS).transpose(2, 0, 1)
    driving = jnp.einsum('fv,nvl->nfl', force_map, host_columns, precision=highest)
    cloud_new = run_clouds(cloud_state, driving, substeps, field_coupling)
    change = (cloud_new - cloud_state).reshape(COLS, FIELDS, LEVELS, CRM_X).mean(axis=3)
    column_tendency = jnp.einsum('vf,nfl->vln', feedback_map, change, precision=highest)
    physics = jnp.broadcast_to(column_tendency.reshape(HVARS, LEVELS, ELEMS, 2, 1, 2, 1), (HVARS, LEVELS, ELEMS, 2, 2, 2, 2)).reshape(HVARS, LEVELS, NODES)
    derivative = jnp.asarray(gll_derivative(), jnp.float32)

    def tendency(field):
        nodes_grid = field.reshape(HVARS, LEVELS, ELEMS, 4, 4)
        along_x = jnp.einsum('ik,vlejk->vleji', derivative, nodes_grid, precision=highest).reshape(field.shape)
        along_y = jnp.einsum('jk,vleki->vleji', derivative, nodes_grid, precision=highest).reshape(field.shape)
        padded = jnp.pad(field, ((0, 0), (1, 1), (0, 0)))
        return -(wind_field[0] * along_x + wind_field[1] * along_y) + host_mix * (padded[:, 2:] + padded[:, :-2] - 2.0 * field) + physics
    mass_total = edge_sum(node_mass.reshape(1, 1, NODES), element_links)

    def smooth(values):
        return edge_sum(node_mass * values, element_links) / mass_total
    first_section = smooth(host_state + host_step * tendency(host_state))
    second_section = smooth(0.75 * host_state + 0.25 * (first_section + host_step * tendency(first_section)))
    host_new = smooth(host_state / 3.0 + 2.0 / 3.0 * (second_section + host_step * tendency(second_section)))
    return (cloud_new, host_new)
```

```python
import functools

import jax
import jax.numpy as jnp
import ml_dtypes
import numpy as np
from jax import lax
from jax.experimental import pallas as pl
from jax.experimental.pallas import tpu as pltpu
from jax.sharding import PartitionSpec as P

CRM_X = 64
HALO = 4
LANES = 128
PAIR = 256

mix = 0.2
cloud_step = 0.1
host_step = 0.1
host_mix = 0.2
bf16 = jnp.bfloat16
f32 = jnp.float32
highest = lax.Precision.HIGHEST
vmem = pl.BlockSpec(memory_space=pltpu.VMEM)
smem = pl.BlockSpec(memory_space=pltpu.SMEM)
params = pltpu.CompilerParams(vmem_limit_bytes=48 * 1024 * 1024)


def gll_derivative():
    points = np.array([-1.0, -1.0 / np.sqrt(5.0), 1.0 / np.sqrt(5.0), 1.0])
    weights = np.array(
        [
            1.0 / np.prod([points[index] - points[other] for other in range(4) if other != index])
            for index in range(4)
        ]
    )
    matrix = np.zeros((4, 4))
    for target in range(4):
        for source in range(4):
            if target != source:
                matrix[target, source] = (
                    weights[source] / weights[target] / (points[target] - points[source])
                )
        matrix[target, target] = -np.sum(matrix[target])
    return matrix


def split(x):
    hi = x.astype(bf16)
    return hi, (x - hi.astype(f32)).astype(bf16)


def mm(a, b):
    return jnp.dot(a, b, preferred_element_type=f32)


def dot_exact_right(x, b):
    hi, lo = split(x)
    return mm(hi, b) + mm(lo, b)


def dot3(a, b):
    a_hi, a_lo = split(a)
    b_hi, b_lo = split(b)
    return mm(a_hi, b_hi) + mm(a_hi, b_lo) + mm(a_lo, b_hi)


def iota(shape, dim):
    return lax.broadcasted_iota(jnp.int32, shape, dim)


def one_hot(cond):
    return jnp.where(cond, 1.0, 0.0).astype(bf16)


def cloud_kernel(
    ends, row_counts, cells, kron, force, feed, columns, out, tend,
    state, spread, k_wide, k_low, parts, change,
):
    rows, n_cells = cells.shape
    half = n_cells // 2
    levels = n_cells // CRM_X
    blocks = half // LANES
    group = 32

    k_hi, k_lo = split(kron[...])
    k_wide[:, :rows] = k_hi
    k_wide[:, rows:] = k_hi
    k_low[...] = k_lo
    driving = cloud_step * dot3(force[...], columns[...])
    src, dst = iota((PAIR, PAIR), 0), iota((PAIR, PAIR), 1)
    weave = one_hot(src == dst % 2 * LANES + dst // LANES * CRM_X + dst % LANES // 2)
    unweave = one_hot(dst == src % 2 * LANES + src // LANES * CRM_X + src % LANES // 2)
    odd = iota((rows, LANES), 1) % 2 == 1

    def ends_of(slot):
        last = state[slot, :, pl.ds(half * 2, LANES)]
        first = state[slot, :, pl.ds(LANES, LANES)]
        state[slot, :, pl.ds(0, LANES)] = jnp.where(odd, pltpu.roll(last, 1, 1), 0.0)
        state[slot, :, pl.ds(half * 2 + LANES, LANES)] = jnp.where(
            odd, 0.0, pltpu.roll(first, LANES - 1, 1)
        )

    def pair_of(ref, k):
        near = pl.multiple_of(k * LANES, LANES)
        far = pl.multiple_of(half + k * LANES, LANES)
        return jnp.concatenate([ref[:, pl.ds(near, LANES)], ref[:, pl.ds(far, LANES)]], axis=1)

    def enter(k, carry):
        at = pl.multiple_of(k * PAIR, LANES)
        state[0, :, pl.ds(pl.multiple_of(at + LANES, LANES), PAIR)] = dot_exact_right(
            pair_of(cells, k), weave
        )
        lane = iota((levels, PAIR), 1)
        level = 2 * k + lane // LANES + lane % 2 * (levels // 2)
        spread[:, pl.ds(at, PAIR)] = dot_exact_right(
            driving, one_hot(iota((levels, PAIR), 0) == level)
        )
        return carry

    lax.fori_loop(0, blocks, enter, 0)
    ends_of(0)

    def step_of(masked):
        def step(s, carry):
            now = s % 2
            later = 1 - now

            def block(k, inner):
                at = pl.multiple_of(k * PAIR, LANES)
                mid = pl.multiple_of(at + LANES, LANES)
                for g in range(0, rows, group):
                    hi, lo = split(state[now, pl.ds(g, group), pl.ds(mid, PAIR)])
                    parts[pl.ds(g, group), :] = hi
                    parts[pl.ds(rows + g, group), :] = lo
                react = mm(k_wide[...], parts[...]) + mm(k_low[...], parts[pl.ds(0, rows), :])
                for g in range(0, rows, group):
                    for c in range(0, PAIR, LANES):
                        take = lambda start: state[
                            now, pl.ds(g, group), pl.ds(pl.multiple_of(start, LANES), LANES)
                        ]
                        x = take(mid + c)
                        total = (x + (take(at + c) + take(mid + c + LANES))) + (
                            pltpu.roll(x, 2, 1) + pltpu.roll(x, LANES - 2, 1)
                        )
                        drive = spread[pl.ds(g, group), pl.ds(pl.multiple_of(at + c, LANES), LANES)]
                        new = mix * total + (
                            cloud_step * jnp.tanh(react[g : g + group, c : c + LANES]) + drive
                        )
                        if masked:
                            new = jnp.where(s < row_counts[pl.ds(g, group), :], new, x)
                        state[
                            later, pl.ds(g, group), pl.ds(pl.multiple_of(mid + c, LANES), LANES)
                        ] = new
                return inner

            lax.fori_loop(0, blocks, block, 0)
            ends_of(later)
            return carry

        return step

    lax.fori_loop(0, ends[0], step_of(False), 0)
    lax.fori_loop(ends[0], ends[1], step_of(True), 0)
    final = ends[1] % 2
    change[...] = jnp.zeros_like(change)

    def leave(k, carry):
        at = pl.multiple_of(k * PAIR + LANES, LANES)
        new = dot_exact_right(state[final, :, pl.ds(at, PAIR)], unweave)
        delta = new - pair_of(cells, k)
        out[:, pl.ds(pl.multiple_of(k * LANES, LANES), LANES)] = new[:, :LANES]
        out[:, pl.ds(pl.multiple_of(half + k * LANES, LANES), LANES)] = new[:, LANES:]
        lane = iota((PAIR, levels), 0)
        level = 2 * k + lane % LANES // CRM_X + lane // LANES * (levels // 2)
        mean = jnp.where(iota((PAIR, levels), 1) == level, 1.0 / CRM_X, 0.0).astype(bf16)
        change[...] += dot_exact_right(delta, mean)
        return carry

    lax.fori_loop(0, blocks, leave, 0)
    tend[...] = dot3(feed[...], change[...])


def spread_diagonal(matrix, count):
    height, width = matrix.shape
    tiled = jnp.tile(matrix, (count, count))
    row = iota(tiled.shape, 0) // height
    col = iota(tiled.shape, 1) // width
    return jnp.where(row == col, tiled, 0.0)


def run_clouds(cloud_state, columns, counts, coupling, force_map, feedback_map):
    own, n_fields, n_cells = cloud_state.shape
    n_vars = columns.shape[1]
    levels = n_cells // CRM_X
    rows = own * n_fields
    ends = jnp.stack([jnp.min(counts), jnp.max(counts)])
    row_counts = jnp.broadcast_to(counts[:, None, None], (own, n_fields, LANES))
    out, tend = pl.pallas_call(
        cloud_kernel,
        out_shape=(
            jax.ShapeDtypeStruct((rows, n_cells), f32),
            jax.ShapeDtypeStruct((own * n_vars, levels), f32),
        ),
        in_specs=[smem] + [vmem] * 6,
        out_specs=(vmem, vmem),
        scratch_shapes=[
            pltpu.VMEM((2, rows, n_cells + 2 * LANES), f32),
            pltpu.VMEM((rows, n_cells), f32),
            pltpu.VMEM((rows, 2 * rows), bf16),
            pltpu.VMEM((rows, rows), bf16),
            pltpu.VMEM((2 * rows, PAIR), bf16),
            pltpu.VMEM((rows, levels), f32),
        ],
        compiler_params=params,
        cost_estimate=pl.CostEstimate(
            flops=2 * 16 * 3 * rows * rows * n_cells,
            bytes_accessed=8 * rows * n_cells,
            transcendentals=16 * rows * n_cells,
        ),
        name="clouds",
    )(
        ends,
        row_counts.reshape(rows, LANES),
        cloud_state.reshape(rows, n_cells),
        spread_diagonal(coupling, own),
        spread_diagonal(force_map, own),
        spread_diagonal(feedback_map, own),
        columns.reshape(own * n_vars, levels),
    )
    return out.reshape(cloud_state.shape), tend.reshape(own, n_vars, levels)


def tables_kernel(sources, masses, gather, remote, inverse, *, elem_dev):
    n = gather.shape[0]
    edge = remote.shape[0] // 2
    node_r, node_c = iota((n, n), 0), iota((n, n), 1)
    own, left, right, vert = (sources[k : k + 1, :] for k in range(4))
    turn = one_hot((node_r == vert) | (node_r == node_c))
    local = one_hot((node_r == own) | (node_r == node_c))
    gather[...] = mm(local, turn).astype(bf16)
    at = iota((edge, n), 0)
    far = jnp.concatenate([one_hot(at == left), one_hot(at == right)], axis=0)
    remote[...] = mm(far, turn).astype(bf16)
    mass = masses[...]
    total = (
        dot_exact_right(mass, gather[...])
        + pltpu.roll(
            dot_exact_right(dot_exact_right(mass, picker(n, 3)), remote[pl.ds(0, edge), :]), 7, 0
        )
        + pltpu.roll(
            dot_exact_right(dot_exact_right(mass, picker(n, 0)), remote[pl.ds(edge, edge), :]), 6, 0
        )
    )
    inverse[...] = jnp.broadcast_to(1.0 / total[:1, :], inverse.shape)


def picker(n, side):
    node, at = iota((n, n // 4), 0), iota((n, n // 4), 1)
    return one_hot(node == at * 4 + side)


def advance(h0, h, wind_x, wind_y, physics, mass, derive, keep, take):
    rows, n = h.shape
    d_hi, d_lo = derive[pl.ds(0, LANES), :], derive[pl.ds(LANES, LANES), :]
    hi, lo = split(h)
    along = []
    for c in range(0, n, LANES):
        a, b = hi[:, c : c + LANES], lo[:, c : c + LANES]
        along.append(mm(a, d_hi) + mm(b, d_hi) + mm(a, d_lo))
    along_x = jnp.concatenate([a[:, :LANES] for a in along], axis=1)
    along_y = jnp.concatenate([a[:, LANES:] for a in along], axis=1)
    tendency = (
        host_mix * (pltpu.roll(h, 1, 0) + pltpu.roll(h, rows - 1, 0) - 2.0 * h)
        - (wind_x * along_x + wind_y * along_y)
        + physics
    )
    value = take * (h + host_step * tendency)
    if keep:
        value = value + keep * h0
    return mass * value


def send_edges(q, to_right, to_left):
    hi, lo = split(q)
    n = q.shape[1]
    right, left = picker(n, 3), picker(n, 0)
    to_right[...] = mm(hi, right) + mm(lo, right)
    to_left[...] = mm(hi, left) + mm(lo, left)


def first_kernel(h0, wind, column, mass, derive, q, to_right, to_left, physics):
    rows, n = h0.shape
    n_cols = column.shape[1]
    node = iota((n_cols, n), 1)
    home = node // 16 * 4 + node // 4 % 4 // 2 * 2 + node % 4 // 2
    physics[...] = dot_exact_right(column[...], one_hot(iota((n_cols, n), 0) == home))
    h = h0[...]
    value = advance(
        h, h, wind[0], wind[1], physics[...], mass[:1, :], derive, 0.0, 1.0
    )
    q[...] = value
    send_edges(value, to_right, to_left)


def joined(q, from_left, from_right, gather, remote, inverse, inside):
    edge = from_left.shape[1]
    total = (
        dot_exact_right(q[...], gather[...])
        + dot_exact_right(from_left[...], remote[pl.ds(0, edge), :])
        + dot_exact_right(from_right[...], remote[pl.ds(edge, edge), :])
    )
    return jnp.where(inside[:, :1] > 0.0, total * inverse[:1, :], 0.0)


def middle_kernel(
    q_in, from_left, from_right, gather, remote, inverse, inside,
    h0, wind, physics, mass, derive, q, to_right, to_left, *, keep, take,
):
    h = joined(q_in, from_left, from_right, gather, remote, inverse, inside)
    value = advance(
        h0[...], h, wind[0], wind[1], physics[...], mass[:1, :], derive, keep, take
    )
    q[...] = value
    send_edges(value, to_right, to_left)


def last_kernel(q_in, from_left, from_right, gather, remote, inverse, inside, out):
    out[...] = joined(q_in, from_left, from_right, gather, remote, inverse, inside)


def call(kernel, shapes, args, name):
    return pl.pallas_call(
        kernel,
        out_shape=tuple(jax.ShapeDtypeStruct(s, t) for s, t in shapes),
        in_specs=[vmem] * len(args),
        out_specs=tuple(vmem for _ in shapes),
        compiler_params=params,
        name=name,
    )(*args)


def shards(
    cloud_state,
    substeps,
    element_links,
    host_state,
    wind_field,
    node_mass,
    field_coupling,
    force_map,
    feedback_map,
):
    own_rows, n_fields, n_cells = cloud_state.shape
    n_vars, lev_dev, n_nodes = host_state.shape
    n_cols = substeps.shape[0]
    elem_dev = n_nodes // 16
    edge = n_nodes // 4
    lev_count = lax.axis_size("lev")
    elem_count = lax.axis_size("elem")
    lev_at = lax.axis_index("lev")
    elem_at = lax.axis_index("elem")
    n_levels = lev_dev * lev_count

    node_ids = jnp.arange(n_nodes)
    column_of_node = node_ids // 16 * 4 + node_ids // 4 % 4 // 2 * 2 + node_ids % 4 // 2
    member = (column_of_node[:, None] == jnp.arange(n_cols)[None, :]).astype(f32)
    host_columns = (
        jnp.dot(host_state.reshape(n_vars * lev_dev, n_nodes), 0.25 * member, precision=highest)
        .reshape(n_vars, lev_dev, n_cols)
        .transpose(2, 0, 1)
    )
    columns = lax.all_to_all(
        host_columns.reshape(lev_count, own_rows, n_vars, lev_dev),
        "lev",
        split_axis=0,
        concat_axis=3,
        tiled=True,
    ).reshape(own_rows, n_vars, n_levels)
    counts = lax.dynamic_slice_in_dim(substeps, lev_at * own_rows, own_rows, 0)

    fields = jnp.concatenate([host_state, wind_field], axis=0)
    up = [(i, i + 1) for i in range(lev_count - 1)]
    down = [(i + 1, i) for i in range(lev_count - 1)]
    fields = jnp.concatenate(
        [
            lax.ppermute(fields[:, lev_dev - HALO :], "lev", up),
            fields,
            lax.ppermute(fields[:, :HALO], "lev", down),
        ],
        axis=1,
    )
    deep = lev_dev + 2 * HALO
    rows = n_vars * deep
    h0 = fields[:n_vars].reshape(rows, n_nodes)
    wind = jnp.tile(fields[n_vars:], (1, n_vars, 1))
    level = lev_at * lev_dev - HALO + jnp.arange(rows) % deep
    inside = jnp.broadcast_to(
        ((level >= 0) & (level < n_levels)).astype(f32)[:, None], (rows, LANES)
    )
    rightward = [(i, (i + 1) % elem_count) for i in range(elem_count)]
    leftward = [((i + 1) % elem_count, i) for i in range(elem_count)]
    masses = jnp.concatenate(
        [
            node_mass[None],
            lax.ppermute(node_mass[None], "elem", rightward),
            lax.ppermute(node_mass[None], "elem", leftward),
            jnp.zeros((5, n_nodes), f32),
        ],
        axis=0,
    )

    ids = jnp.arange(n_nodes, dtype=jnp.int32)
    row_of, col_of = ids // 4 % 4, ids % 4
    links = jnp.repeat(element_links.T, 16, axis=1)
    here = links // elem_dev == elem_at
    place = links % elem_dev
    side_own = jnp.where(
        (col_of == 0) & here[0],
        place[0] * 16 + row_of * 4 + 3,
        jnp.where((col_of == 3) & here[1], place[1] * 16 + row_of * 4, -1),
    )
    side_left = jnp.where((col_of == 0) & ~here[0], place[0] * 4 + row_of, -1)
    side_right = jnp.where((col_of == 3) & ~here[1], place[1] * 4 + row_of, -1)
    vert = jnp.where(
        row_of == 0,
        place[2] * 16 + 12 + col_of,
        jnp.where(row_of == 3, place[3] * 16 + col_of, -1),
    )
    none = jnp.full_like(vert, -1)
    sources = jnp.stack([side_own, side_left, side_right, vert, none, none, none, none])
    gather, remote, inverse = call(
        functools.partial(tables_kernel, elem_dev=elem_dev),
        [((n_nodes, n_nodes), bf16), ((2 * edge, n_nodes), bf16), ((8, n_nodes), f32)],
        (sources, masses),
        "tables",
    )

    cloud_new, tend = run_clouds(
        cloud_state, columns, counts, field_coupling, force_map, feedback_map
    )

    padded = jnp.pad(tend, ((0, 0), (0, 0), (HALO, HALO)))
    blocks = jnp.stack(
        [padded[:, :, k * lev_dev : k * lev_dev + deep] for k in range(lev_count)]
    )
    column = (
        lax.all_to_all(blocks, "lev", split_axis=0, concat_axis=0, tiled=True)
        .reshape(n_cols, rows)
        .T
    )

    derivative = gll_derivative()
    elems = LANES // 16
    derive = np.concatenate(
        [
            np.kron(np.eye(elems * 4), derivative).T,
            np.kron(np.eye(elems), np.kron(derivative, np.eye(4))).T,
        ],
        axis=1,
    ).astype(np.float32)
    d_hi = derive.astype(ml_dtypes.bfloat16)
    d_lo = (derive - d_hi.astype(np.float32)).astype(ml_dtypes.bfloat16)
    derive = jnp.asarray(np.concatenate([d_hi, d_lo], axis=0))

    q_shapes = [((rows, n_nodes), f32), ((rows, edge), f32), ((rows, edge), f32)]
    q, to_right, to_left, physics = call(
        first_kernel,
        q_shapes + [((rows, n_nodes), f32)],
        (h0, wind, column, masses, derive),
        "first",
    )
    for keep, take in ((0.75, 0.25), (1.0 / 3.0, 2.0 / 3.0)):
        from_left = lax.ppermute(to_right, "elem", rightward)
        from_right = lax.ppermute(to_left, "elem", leftward)
        q, to_right, to_left = call(
            functools.partial(middle_kernel, keep=keep, take=take),
            q_shapes,
            (q, from_left, from_right, gather, remote, inverse, inside, h0, wind, physics, masses,
             derive),
            "middle",
        )
    from_left = lax.ppermute(to_right, "elem", rightward)
    from_right = lax.ppermute(to_left, "elem", leftward)
    (last,) = call(
        last_kernel,
        [((rows, n_nodes), f32)],
        (q, from_left, from_right, gather, remote, inverse, inside),
        "last",
    )
    host_new = last.reshape(n_vars, deep, n_nodes)[:, HALO : HALO + lev_dev]
    return (cloud_new, host_new)


def solution(mesh):
    placed = (
        P(("elem", "lev"), None, None),
        P("elem"),
        P("elem", None),
        P(None, "lev", "elem"),
        P(None, "lev", "elem"),
        P("elem"),
        P(),
        P(),
        P(),
    )
    return jax.shard_map(
        shards,
        mesh=mesh,
        in_specs=placed,
        out_specs=(P(("elem", "lev"), None, None), P(None, "lev", "elem")),
        check_vma=False,
    )
```

```python
import functools

import jax
import jax.numpy as jnp
import ml_dtypes
import numpy as np
from jax import lax
from jax.experimental import pallas as pl
from jax.experimental.pallas import tpu as pltpu
from jax.sharding import PartitionSpec as P

CRM_X = 64
HALO = 4
LANES = 128
PAIR = 256
GROUP = 32
UNROLL = 2

mix = 0.2
cloud_step = 0.1
host_step = 0.1
host_mix = 0.2
bf16 = jnp.bfloat16
f32 = jnp.float32
highest = lax.Precision.HIGHEST
vmem = pl.BlockSpec(memory_space=pltpu.VMEM)
smem = pl.BlockSpec(memory_space=pltpu.SMEM)
params = pltpu.CompilerParams(vmem_limit_bytes=48 * 1024 * 1024)


def gll_derivative():
    points = np.array([-1.0, -1.0 / np.sqrt(5.0), 1.0 / np.sqrt(5.0), 1.0])
    weights = np.array(
        [
            1.0 / np.prod([points[index] - points[other] for other in range(4) if other != index])
            for index in range(4)
        ]
    )
    matrix = np.zeros((4, 4))
    for target in range(4):
        for source in range(4):
            if target != source:
                matrix[target, source] = (
                    weights[source] / weights[target] / (points[target] - points[source])
                )
        matrix[target, target] = -np.sum(matrix[target])
    return matrix


def split(x):
    hi = x.astype(bf16)
    return hi, (x - hi.astype(f32)).astype(bf16)


def mm(a, b):
    return jnp.dot(a, b, preferred_element_type=f32)


def dot_exact_right(x, b):
    hi, lo = split(x)
    return mm(hi, b) + mm(lo, b)


def iota(shape, dim):
    return lax.broadcasted_iota(jnp.int32, shape, dim)


def one_hot(cond):
    return jnp.where(cond, 1.0, 0.0).astype(bf16)


def diagonal(matrix, height, width, part, rows, cols):
    piece = split(matrix[...])[part]
    down = one_hot(iota((rows, LANES), 1) == iota((rows, LANES), 0) % height)
    along = one_hot(iota((LANES, cols), 0) == iota((LANES, cols), 1) % width)
    tiled = mm(mm(down, piece).astype(bf16), along)
    same = iota((rows, cols), 0) // height == iota((rows, cols), 1) // width
    return jnp.where(same, tiled, 0.0).astype(bf16)


def cloud_kernel(
    fields, n_vars, ends, row_counts, cells, kron, force, feed, columns, out, tend,
    state, other, spread, k_wide, k_low, change,
):
    rows, n_cells = cells.shape
    half = n_cells // 2
    levels = n_cells // CRM_X
    blocks = half // LANES
    k_hi, k_lo = (diagonal(kron, fields, fields, part, rows, rows) for part in (0, 1))
    k_wide[:, :rows] = k_hi
    k_wide[:, rows:] = k_hi
    k_low[...] = k_lo
    wide = columns.shape[0]
    f_hi, f_lo = (diagonal(force, fields, n_vars, part, rows, wide) for part in (0, 1))
    c_hi, c_lo = split(columns[...])
    driving = cloud_step * (mm(f_hi, c_hi) + mm(f_hi, c_lo) + mm(f_lo, c_hi))
    src, dst = iota((PAIR, PAIR), 0), iota((PAIR, PAIR), 1)
    weave = one_hot(src == dst % 2 * LANES + dst // LANES * CRM_X + dst % LANES // 2)
    unweave = one_hot(dst == src % 2 * LANES + src // LANES * CRM_X + src % LANES // 2)
    odd = iota((rows, LANES), 1) % 2 == 1

    def ends_of(ref):
        last = ref[:, pl.ds(half * 2, LANES)]
        first = ref[:, pl.ds(LANES, LANES)]
        ref[:, pl.ds(0, LANES)] = jnp.where(odd, pltpu.roll(last, 1, 1), 0.0)
        ref[:, pl.ds(half * 2 + LANES, LANES)] = jnp.where(
            odd, 0.0, pltpu.roll(first, LANES - 1, 1)
        )

    def pair_of(ref, k):
        near = pl.multiple_of(k * LANES, LANES)
        far = pl.multiple_of(half + k * LANES, LANES)
        return jnp.concatenate([ref[:, pl.ds(near, LANES)], ref[:, pl.ds(far, LANES)]], axis=1)

    def enter(k, carry):
        at = pl.multiple_of(k * PAIR, LANES)
        state[:, pl.ds(pl.multiple_of(at + LANES, LANES), PAIR)] = dot_exact_right(
            pair_of(cells, k), weave
        )
        lane = iota((levels, PAIR), 1)
        level = 2 * k + lane // LANES + lane % 2 * (levels // 2)
        spread[:, pl.ds(at, PAIR)] = dot_exact_right(
            driving, one_hot(iota((levels, PAIR), 0) == level)
        )
        return carry

    lax.fori_loop(0, blocks, enter, 0, unroll=UNROLL)
    ends_of(state)

    def step(now, later, s, masked):
        def block(k, inner):
            at = pl.multiple_of(k * PAIR, LANES)
            mid = pl.multiple_of(at + LANES, LANES)
            hi, lo = split(now[:, pl.ds(mid, PAIR)])
            react = mm(k_wide[...], jnp.concatenate([hi, lo], axis=0)) + mm(k_low[...], hi)
            for g in range(0, rows, GROUP):
                own = pl.ds(g, min(GROUP, rows))
                x = now[own, pl.ds(mid, PAIR)]
                beside = jnp.concatenate(
                    [
                        pltpu.roll(x[:, c : c + LANES], 2, 1)
                        + pltpu.roll(x[:, c : c + LANES], LANES - 2, 1)
                        for c in range(0, PAIR, LANES)
                    ],
                    axis=1,
                )
                below = now[own, pl.ds(at, PAIR)]
                above = now[own, pl.ds(pl.multiple_of(mid + LANES, LANES), PAIR)]
                total = (x + (below + above)) + beside
                new = mix * total + (
                    cloud_step * jnp.tanh(react[g : g + GROUP]) + spread[own, pl.ds(at, PAIR)]
                )
                if masked:
                    alive = s < row_counts[own, :]
                    new = jnp.where(jnp.concatenate([alive] * (PAIR // LANES), axis=1), new, x)
                later[own, pl.ds(mid, PAIR)] = new
            return inner

        lax.fori_loop(0, blocks, block, 0, unroll=UNROLL)
        ends_of(later)

    def steps_of(masked):
        def two(pair, carry):
            step(state, other, 2 * pair, masked)
            step(other, state, 2 * pair + 1, masked)
            return carry

        return two

    full = ends[0] // 2
    lax.fori_loop(0, full, steps_of(False), 0)
    lax.fori_loop(full, (ends[1] + 1) // 2, steps_of(True), 0)
    change[...] = jnp.zeros_like(change)

    def leave(k, carry):
        at = pl.multiple_of(k * PAIR + LANES, LANES)
        new = dot_exact_right(state[:, pl.ds(at, PAIR)], unweave)
        delta = new - pair_of(cells, k)
        out[:, pl.ds(pl.multiple_of(k * LANES, LANES), LANES)] = new[:, :LANES]
        out[:, pl.ds(pl.multiple_of(half + k * LANES, LANES), LANES)] = new[:, LANES:]
        lane = iota((PAIR, levels), 0)
        level = 2 * k + lane % LANES // CRM_X + lane // LANES * (levels // 2)
        mean = jnp.where(iota((PAIR, levels), 1) == level, 1.0 / CRM_X, 0.0).astype(bf16)
        change[...] += dot_exact_right(delta, mean)
        return carry

    lax.fori_loop(0, blocks, leave, 0, unroll=UNROLL)
    b_hi, b_lo = (diagonal(feed, n_vars, fields, part, wide, rows) for part in (0, 1))
    d_hi, d_lo = split(change[...])
    tend[...] = mm(b_hi, d_hi) + mm(b_hi, d_lo) + mm(b_lo, d_hi)


def square(matrix):
    height, width = matrix.shape
    return jnp.pad(matrix, ((0, LANES - height), (0, LANES - width)))


def run_clouds(cloud_state, columns, counts, coupling, force_map, feedback_map):
    own, n_fields, n_cells = cloud_state.shape
    n_vars = columns.shape[1]
    levels = n_cells // CRM_X
    rows = own * n_fields
    ends = jnp.stack([jnp.min(counts), jnp.max(counts)])
    row_counts = jnp.broadcast_to(counts[:, None, None], (own, n_fields, LANES))
    out, tend = pl.pallas_call(
        functools.partial(cloud_kernel, n_fields, n_vars),
        out_shape=(
            jax.ShapeDtypeStruct((rows, n_cells), f32),
            jax.ShapeDtypeStruct((own * n_vars, levels), f32),
        ),
        in_specs=[smem] + [vmem] * 6,
        out_specs=(vmem, vmem),
        scratch_shapes=[
            pltpu.VMEM((rows, n_cells + 2 * LANES), f32),
            pltpu.VMEM((rows, n_cells + 2 * LANES), f32),
            pltpu.VMEM((rows, n_cells), f32),
            pltpu.VMEM((rows, 2 * rows), bf16),
            pltpu.VMEM((rows, rows), bf16),
            pltpu.VMEM((rows, levels), f32),
        ],
        compiler_params=params,
        cost_estimate=pl.CostEstimate(
            flops=2 * 16 * 3 * rows * rows * n_cells,
            bytes_accessed=8 * rows * n_cells,
            transcendentals=16 * rows * n_cells,
        ),
        name="clouds",
    )(
        ends,
        row_counts.reshape(rows, LANES),
        cloud_state.reshape(rows, n_cells),
        square(coupling),
        square(force_map),
        square(feedback_map),
        columns.reshape(own * n_vars, levels),
    )
    return out.reshape(cloud_state.shape), tend.reshape(own, n_vars, levels)


def tables_kernel(sources, masses, gather, remote, inverse, *, elem_dev):
    n = gather.shape[0]
    edge = remote.shape[0] // 2
    node_r, node_c = iota((n, n), 0), iota((n, n), 1)
    own, left, right, vert = (sources[k : k + 1, :] for k in range(4))
    turn = one_hot((node_r == vert) | (node_r == node_c))
    local = one_hot((node_r == own) | (node_r == node_c))
    gather[...] = mm(local, turn).astype(bf16)
    at = iota((edge, n), 0)
    far = jnp.concatenate([one_hot(at == left), one_hot(at == right)], axis=0)
    remote[...] = mm(far, turn).astype(bf16)
    mass = masses[...]
    total = (
        dot_exact_right(mass, gather[...])
        + pltpu.roll(
            dot_exact_right(dot_exact_right(mass, picker(n, 3)), remote[pl.ds(0, edge), :]), 7, 0
        )
        + pltpu.roll(
            dot_exact_right(dot_exact_right(mass, picker(n, 0)), remote[pl.ds(edge, edge), :]), 6, 0
        )
    )
    inverse[...] = jnp.broadcast_to(1.0 / total[:1, :], inverse.shape)


def picker(n, side):
    node, at = iota((n, n // 4), 0), iota((n, n // 4), 1)
    return one_hot(node == at * 4 + side)


def advance(h0, h, wind_x, wind_y, physics, mass, derive, keep, take):
    rows, n = h.shape
    d_hi, d_lo = derive[pl.ds(0, LANES), :], derive[pl.ds(LANES, LANES), :]
    hi, lo = split(h)
    along = []
    for c in range(0, n, LANES):
        a, b = hi[:, c : c + LANES], lo[:, c : c + LANES]
        along.append(mm(a, d_hi) + mm(b, d_hi) + mm(a, d_lo))
    along_x = jnp.concatenate([a[:, :LANES] for a in along], axis=1)
    along_y = jnp.concatenate([a[:, LANES:] for a in along], axis=1)
    tendency = (
        host_mix * (pltpu.roll(h, 1, 0) + pltpu.roll(h, rows - 1, 0) - 2.0 * h)
        - (wind_x * along_x + wind_y * along_y)
        + physics
    )
    value = take * (h + host_step * tendency)
    if keep:
        value = value + keep * h0
    return mass * value


def send_edges(q, to_right, to_left):
    hi, lo = split(q)
    n = q.shape[1]
    right, left = picker(n, 3), picker(n, 0)
    to_right[...] = mm(hi, right) + mm(lo, right)
    to_left[...] = mm(hi, left) + mm(lo, left)


def first_kernel(h0, wind, column, mass, derive, q, to_right, to_left, physics):
    rows, n = h0.shape
    n_cols = column.shape[1]
    node = iota((n_cols, n), 1)
    home = node // 16 * 4 + node // 4 % 4 // 2 * 2 + node % 4 // 2
    physics[...] = dot_exact_right(column[...], one_hot(iota((n_cols, n), 0) == home))
    h = h0[...]
    value = advance(
        h, h, wind[0], wind[1], physics[...], mass[:1, :], derive, 0.0, 1.0
    )
    q[...] = value
    send_edges(value, to_right, to_left)


def joined(q, from_left, from_right, gather, remote, inverse, inside):
    edge = from_left.shape[1]
    total = (
        dot_exact_right(q[...], gather[...])
        + dot_exact_right(from_left[...], remote[pl.ds(0, edge), :])
        + dot_exact_right(from_right[...], remote[pl.ds(edge, edge), :])
    )
    return jnp.where(inside[:, :1] > 0.0, total * inverse[:1, :], 0.0)


def middle_kernel(
    q_in, from_left, from_right, gather, remote, inverse, inside,
    h0, wind, physics, mass, derive, q, to_right, to_left, *, keep, take,
):
    h = joined(q_in, from_left, from_right, gather, remote, inverse, inside)
    value = advance(
        h0[...], h, wind[0], wind[1], physics[...], mass[:1, :], derive, keep, take
    )
    q[...] = value
    send_edges(value, to_right, to_left)


def last_kernel(q_in, from_left, from_right, gather, remote, inverse, inside, out):
    out[...] = joined(q_in, from_left, from_right, gather, remote, inverse, inside)


def call(kernel, shapes, args, name):
    return pl.pallas_call(
        kernel,
        out_shape=tuple(jax.ShapeDtypeStruct(s, t) for s, t in shapes),
        in_specs=[vmem] * len(args),
        out_specs=tuple(vmem for _ in shapes),
        compiler_params=params,
        name=name,
    )(*args)


def shards(
    cloud_state,
    substeps,
    element_links,
    host_state,
    wind_field,
    node_mass,
    field_coupling,
    force_map,
    feedback_map,
):
    own_rows, n_fields, n_cells = cloud_state.shape
    n_vars, lev_dev, n_nodes = host_state.shape
    n_cols = substeps.shape[0]
    elem_dev = n_nodes // 16
    edge = n_nodes // 4
    lev_count = lax.axis_size("lev")
    elem_count = lax.axis_size("elem")
    lev_at = lax.axis_index("lev")
    elem_at = lax.axis_index("elem")
    n_levels = lev_dev * lev_count

    node_ids = jnp.arange(n_nodes)
    column_of_node = node_ids // 16 * 4 + node_ids // 4 % 4 // 2 * 2 + node_ids % 4 // 2
    member = (column_of_node[:, None] == jnp.arange(n_cols)[None, :]).astype(f32)
    host_columns = (
        jnp.dot(host_state.reshape(n_vars * lev_dev, n_nodes), 0.25 * member, precision=highest)
        .reshape(n_vars, lev_dev, n_cols)
        .transpose(2, 0, 1)
    )
    columns = lax.all_to_all(
        host_columns.reshape(lev_count, own_rows, n_vars, lev_dev),
        "lev",
        split_axis=0,
        concat_axis=3,
        tiled=True,
    ).reshape(own_rows, n_vars, n_levels)
    counts = lax.dynamic_slice_in_dim(substeps, lev_at * own_rows, own_rows, 0)

    fields = jnp.concatenate([host_state, wind_field], axis=0)
    up = [(i, i + 1) for i in range(lev_count - 1)]
    down = [(i + 1, i) for i in range(lev_count - 1)]
    fields = jnp.concatenate(
        [
            lax.ppermute(fields[:, lev_dev - HALO :], "lev", up),
            fields,
            lax.ppermute(fields[:, :HALO], "lev", down),
        ],
        axis=1,
    )
    deep = lev_dev + 2 * HALO
    rows = n_vars * deep
    h0 = fields[:n_vars].reshape(rows, n_nodes)
    wind = jnp.tile(fields[n_vars:], (1, n_vars, 1))
    level = lev_at * lev_dev - HALO + jnp.arange(rows) % deep
    inside = jnp.broadcast_to(
        ((level >= 0) & (level < n_levels)).astype(f32)[:, None], (rows, LANES)
    )
    rightward = [(i, (i + 1) % elem_count) for i in range(elem_count)]
    leftward = [((i + 1) % elem_count, i) for i in range(elem_count)]
    masses = jnp.concatenate(
        [
            node_mass[None],
            lax.ppermute(node_mass[None], "elem", rightward),
            lax.ppermute(node_mass[None], "elem", leftward),
            jnp.zeros((5, n_nodes), f32),
        ],
        axis=0,
    )

    ids = jnp.arange(n_nodes, dtype=jnp.int32)
    row_of, col_of = ids // 4 % 4, ids % 4
    links = jnp.repeat(element_links.T, 16, axis=1)
    here = links // elem_dev == elem_at
    place = links % elem_dev
    side_own = jnp.where(
        (col_of == 0) & here[0],
        place[0] * 16 + row_of * 4 + 3,
        jnp.where((col_of == 3) & here[1], place[1] * 16 + row_of * 4, -1),
    )
    side_left = jnp.where((col_of == 0) & ~here[0], place[0] * 4 + row_of, -1)
    side_right = jnp.where((col_of == 3) & ~here[1], place[1] * 4 + row_of, -1)
    vert = jnp.where(
        row_of == 0,
        place[2] * 16 + 12 + col_of,
        jnp.where(row_of == 3, place[3] * 16 + col_of, -1),
    )
    none = jnp.full_like(vert, -1)
    sources = jnp.stack([side_own, side_left, side_right, vert, none, none, none, none])
    gather, remote, inverse = call(
        functools.partial(tables_kernel, elem_dev=elem_dev),
        [((n_nodes, n_nodes), bf16), ((2 * edge, n_nodes), bf16), ((8, n_nodes), f32)],
        (sources, masses),
        "tables",
    )

    cloud_new, tend = run_clouds(
        cloud_state, columns, counts, field_coupling, force_map, feedback_map
    )

    padded = jnp.pad(tend, ((0, 0), (0, 0), (HALO, HALO)))
    blocks = jnp.stack(
        [padded[:, :, k * lev_dev : k * lev_dev + deep] for k in range(lev_count)]
    )
    column = (
        lax.all_to_all(blocks, "lev", split_axis=0, concat_axis=0, tiled=True)
        .reshape(n_cols, rows)
        .T
    )

    derivative = gll_derivative()
    elems = LANES // 16
    derive = np.concatenate(
        [
            np.kron(np.eye(elems * 4), derivative).T,
            np.kron(np.eye(elems), np.kron(derivative, np.eye(4))).T,
        ],
        axis=1,
    ).astype(np.float32)
    d_hi = derive.astype(ml_dtypes.bfloat16)
    d_lo = (derive - d_hi.astype(np.float32)).astype(ml_dtypes.bfloat16)
    derive = jnp.asarray(np.concatenate([d_hi, d_lo], axis=0))

    q_shapes = [((rows, n_nodes), f32), ((rows, edge), f32), ((rows, edge), f32)]
    q, to_right, to_left, physics = call(
        first_kernel,
        q_shapes + [((rows, n_nodes), f32)],
        (h0, wind, column, masses, derive),
        "first",
    )
    for keep, take in ((0.75, 0.25), (1.0 / 3.0, 2.0 / 3.0)):
        from_left = lax.ppermute(to_right, "elem", rightward)
        from_right = lax.ppermute(to_left, "elem", leftward)
        q, to_right, to_left = call(
            functools.partial(middle_kernel, keep=keep, take=take),
            q_shapes,
            (q, from_left, from_right, gather, remote, inverse, inside, h0, wind, physics, masses,
             derive),
            "middle",
        )
    from_left = lax.ppermute(to_right, "elem", rightward)
    from_right = lax.ppermute(to_left, "elem", leftward)
    (last,) = call(
        last_kernel,
        [((rows, n_nodes), f32)],
        (q, from_left, from_right, gather, remote, inverse, inside),
        "last",
    )
    host_new = last.reshape(n_vars, deep, n_nodes)[:, HALO : HALO + lev_dev]
    return (cloud_new, host_new)


def solution(mesh):
    placed = (
        P(("elem", "lev"), None, None),
        P("elem"),
        P("elem", None),
        P(None, "lev", "elem"),
        P(None, "lev", "elem"),
        P("elem"),
        P(),
        P(),
        P(),
    )
    return jax.shard_map(
        shards,
        mesh=mesh,
        in_specs=placed,
        out_specs=(P(("elem", "lev"), None, None), P(None, "lev", "elem")),
        check_vma=False,
    )
```
